128 devices in a mesh: dp: 8 (over x, core), tensor: 16 (over z, y).
Axes of the slice: x: 4, y: 4, z: 4, core: 2. Of those that a mesh axis runs over, the one named last changes fastest.
Arguments:
- hidden: bfloat16 [1024, 53248], P('dp', 'tensor'), may hold values from -6 to 6
- out_grad: bfloat16 [1024, 8192], P('dp'), may hold values from -4 to 4
- weight: bfloat16 [53248, 8192], P('tensor', 'dp'), may hold values from -0.02734375 to 0.02734375
- inv_scale: float32 [8192], P('dp'), may hold values from 392.28397 to 1199.9275
Outputs:
- hidden_grad: bfloat16 [1024, 53248], P('dp', 'tensor')
- weight_grad: bfloat16 [53248, 8192], P('tensor', 'dp')
The draws below stay inside these ranges and needn't reach their ends.
All inputs are finite; a program needn't handle non-finite values.
Results may differ from the reference program's by a relative error of at most 0.02.
Values may be sent and summed in bfloat16 or wider, within the bound.
No kernel may reach another device: no remote copies, remote signals or barrier semaphores. Data moves between devices by JAX's collectives and lax.ppermute only.
A program may use at most 128 MiB of HBM per device.

```python
import math
import jax
import jax.numpy as jnp
from jax import lax

D = 8192
FF = 53248
HB = 256
TOKENS = 1024
N_DP = 8
N_TENSOR = 16


def shard_levels(own_key, shape, split, least, largest):
    gain, own = 1.0, jax.random.fold_in(own_key, 6)
    for dim, shards_of in split:
        heights = jnp.exp(jax.random.uniform(jax.random.fold_in(own, dim), (shards_of,), jnp.float32, least / len(split), largest / len(split)))
        gain = gain * jnp.repeat(heights, shape[dim] // shards_of).reshape([-1 if axis == dim else 1 for axis in range(len(shape))])
    return gain


def centred(key, extent, scale, bound, shards=(), kind=jnp.bfloat16):
    result = scale * jax.random.normal(key, extent, jnp.float32)
    if shards:
        result = result * shard_levels(key, extent, shards, -0.22, 0.18)
    return jnp.clip(result, -bound, bound).astype(kind)


def setup_inputs(seed: int = 0) -> dict:
    keys = jax.random.split(jax.random.key(seed), 5)
    return {
        "hidden": centred(keys[0], (TOKENS, FF), 1.0, 6.0, ((0, 8), (1, 16))),
        "out_grad": centred(keys[1], (TOKENS, D), 0.3, 4.0, ((0, 8),)),
        "weight": centred(keys[2], (FF, D), FF ** -0.5, 0.02734375, ((0, 16), (1, 8))),
        "inv_scale": jnp.clip(jnp.exp(math.log(1199.9275) - 1.1180304 * jax.random.uniform(keys[3], (D,), jnp.float32) ** shard_levels(keys[3], (D,), ((0, 8),), -0.2, 0.2)), 392.28397, 1199.9275),
    }


def hadamard(order_size):
    indices = jnp.arange(order_size, dtype=jnp.int32)
    parity = jnp.zeros((order_size, order_size), jnp.int32)
    bit_pos = 0
    while 1 << bit_pos < order_size:
        parity = parity + jnp.bitwise_and(jnp.right_shift(indices[:, None], bit_pos), 1) * jnp.bitwise_and(jnp.right_shift(indices[None, :], bit_pos), 1)
        bit_pos = bit_pos + 1
    return (1 - 2 * (parity % 2)).astype(jnp.float32)

def transform(values):
    tok_rows = values.shape[0]
    cross_table = hadamard(N_TENSOR)
    block_table = hadamard(HB)
    blocks = values.reshape(tok_rows, N_TENSOR, FF // N_TENSOR)
    blocks = jnp.einsum('rjw,sj->rsw', blocks, cross_table, precision=lax.Precision.HIGHEST)
    blocks = blocks.reshape(tok_rows, N_TENSOR, FF // N_TENSOR // HB, HB)
    blocks = jnp.einsum('rsbk,kl->rsbl', blocks, block_table, precision=lax.Precision.HIGHEST)
    return blocks.reshape(tok_rows, FF) * (1.0 / math.sqrt(N_TENSOR * HB))

def reference(hidden, out_grad, weight, inv_scale):
    rotated = transform(hidden.astype(jnp.float32)).astype(jnp.bfloat16)
    group_cols = D // N_DP
    weight_blocks = weight.reshape(FF, N_DP, group_cols).transpose(1, 0, 2)
    inv_blocks = inv_scale.reshape(N_DP, group_cols)
    grad_blocks = out_grad.reshape(TOKENS, N_DP, group_cols).transpose(1, 0, 2)

    def quant_step(running_sum, blocks_in):
        weight_block, inv_block, grad_block = blocks_in
        raw_code = jnp.floor(weight_block.astype(jnp.float32) * inv_block[None, :] + 0.5)
        keep_mask = jnp.logical_and(raw_code >= -8.0, raw_code <= 7.0)
        quant_weight = (jnp.clip(raw_code, -8.0, 7.0) / inv_block[None, :]).astype(jnp.bfloat16)
        partial_grad = lax.dot_general(grad_block, quant_weight, (((1,), (1,)), ((), ())), preferred_element_type=jnp.float32).astype(jnp.bfloat16)
        running_sum = running_sum + partial_grad.astype(jnp.float32)
        weight_sum = lax.dot_general(rotated, grad_block, (((0,), (0,)), ((), ())), preferred_element_type=jnp.float32)
        weight_part = jnp.where(keep_mask, weight_sum, 0.0).astype(jnp.bfloat16)
        return (running_sum, weight_part)
    start_sum = jnp.zeros((TOKENS, FF), jnp.float32)
    rotated_grad, weight_parts = lax.scan(quant_step, start_sum, (weight_blocks, inv_blocks, grad_blocks))
    weight_grad = weight_parts.transpose(1, 0, 2).reshape(FF, D)
    hidden_grad = transform(rotated_grad).astype(jnp.bfloat16)
    return (hidden_grad, weight_grad)
```

```python
import jax
import jax.numpy as jnp
from jax import lax
from jax.sharding import PartitionSpec as P

HB = 256
AXES = ("x", "core", "z", "y")
BF16 = jnp.bfloat16
F32 = jnp.float32


def move(value, route):
    nx, nc, nz, ny = (lax.axis_size(axis) for axis in AXES)

    def flat(x, c, z, y):
        return ((x % nx * nc + c) * nz + z) * ny + y

    pairs = [
        (flat(x, c, z, y), flat(*route(x, c, z, y)))
        for x in range(nx)
        for c in range(nc)
        for z in range(nz)
        for y in range(ny)
    ]
    return lax.ppermute(value, AXES, pairs)


def swap(value):
    return move(value, lambda x, c, z, y: (x, 1 - c, z, y))


def forward(value):
    return move(value, lambda x, c, z, y: (x + 1 - 2 * c, c, z, y))


def backward(value):
    return move(value, lambda x, c, z, y: (x - 1 + 2 * c, c, z, y))


def across(value):
    return move(value, lambda x, c, z, y: (x + 2, c, z, y))


def hadamard(order):
    i = jnp.arange(order, dtype=jnp.int32)
    both = jnp.bitwise_and(i[:, None], i[None, :])
    return (1 - 2 * (lax.population_count(both) % 2)).astype(BF16)


def mix_blocks(value):
    core, z, y = (lax.axis_index(axis) for axis in ("core", "z", "y"))
    for step in range(4):
        bit = 1 << (step % 2)
        y_first = step < 2

        def route(x, c, zz, yy, bit=bit, y_first=y_first):
            return (x, c, zz, yy ^ bit) if (c == 0) == y_first else (x, c, zz ^ bit, yy)

        partner = move(value, route)
        place = jnp.where((core == 0) == y_first, y, z)
        sign = jnp.where(jnp.bitwise_and(place, bit) == 0, 1.0, -1.0).astype(F32)
        total = value.astype(F32) * sign + partner.astype(F32)
        value = total.astype(BF16) if step < 3 else total
    return value


def on_device(hidden, out_grad, weight, inv_scale):
    x, core = lax.axis_index("x"), lax.axis_index("core")
    table = hadamard(HB)
    scaling = 1.0 / 64.0
    tokens, ff = hidden.shape
    cols = weight.shape[1]

    def columns(distance):
        chip = lax.rem(x + distance + 4, 4)
        return lax.dynamic_slice(out_grad, (0, chip * 2 * cols), (tokens, 2 * cols))

    def halves(value):
        mine = lax.dynamic_slice(value, (0, core * cols), (tokens, cols))
        other = lax.dynamic_slice(value, (0, (1 - core) * cols), (tokens, cols))
        return mine, other

    ahead = 1 - 2 * core
    from_across = across(columns(2))
    from_fwd = backward(columns(-ahead))
    from_bwd = forward(columns(ahead))
    own_mine, own_send = halves(columns(0))
    across_mine, across_send = halves(from_across)
    fwd_mine, fwd_send = halves(from_fwd)
    bwd_mine, bwd_send = halves(from_bwd)
    own_other, across_other = swap(own_send), swap(across_send)
    fwd_other, bwd_other = swap(bwd_send), swap(fwd_send)

    raw_code = jnp.floor(weight.astype(F32) * inv_scale[None, :] + 0.5)
    code = jnp.clip(raw_code, -8.0, 7.0).astype(BF16)
    turned = jnp.einsum(
        "kl,bkd->bld", table, code.reshape(ff // HB, HB, cols), preferred_element_type=F32
    ).reshape(ff, cols)
    turned = (turned * (scaling / inv_scale)[None, :]).astype(BF16)

    def product(mine, other):
        both = lax.dot_general(
            jnp.concatenate([mine, other]),
            turned,
            (((1,), (1,)), ((), ())),
            preferred_element_type=F32,
        ).astype(BF16)
        return both[:tokens], both[tokens:]

    def add(*terms):
        return sum(term.astype(F32) for term in terms).astype(BF16)

    p_across = product(across_mine, across_other)
    first = forward(add(p_across[0], swap(p_across[1])))
    p_fwd = product(fwd_mine, fwd_other)
    p_bwd = product(bwd_mine, bwd_other)
    second = forward(add(p_fwd[1], swap(p_bwd[0])))
    third = forward(add(p_fwd[0], swap(p_bwd[1]), first))
    p_own = product(own_mine, own_other)
    grad = add(p_own[0], swap(p_own[1]), swap(second), third)
    hidden_grad = mix_blocks(grad).astype(BF16)

    mixed = mix_blocks(hidden).astype(BF16)
    rotated = lax.dot_general(
        mixed.reshape(tokens * ff // HB, HB), table, (((1,), (0,)), ((), ())), preferred_element_type=F32
    )
    rotated = (rotated * scaling).astype(BF16).reshape(tokens, ff)
    other = swap(rotated)
    bwd_a = forward(rotated)
    bwd_b = forward(other)
    opp_a = forward(bwd_a)
    every = [rotated, other, bwd_a, bwd_b, swap(bwd_b), swap(bwd_a), opp_a, swap(opp_a)]
    grads = [own_mine, own_other, bwd_mine, bwd_other, fwd_mine, fwd_other, across_mine, across_other]
    weight_sum = lax.dot_general(
        jnp.concatenate(every),
        jnp.concatenate(grads),
        (((0,), (0,)), ((), ())),
        preferred_element_type=F32,
    )
    keep = jnp.logical_and(raw_code >= -8.0, raw_code <= 7.0)
    weight_grad = jnp.where(keep, weight_sum, 0.0).astype(BF16)
    return hidden_grad, weight_grad


def solution(mesh):
    grid = jax.sharding.Mesh(mesh.devices.reshape(4, 2, 4, 4), AXES)
    dp, tensor = ("x", "core"), ("z", "y")
    in_specs = (P(dp, tensor), P(dp, None), P(tensor, dp), P(dp))
    out_specs = (P(dp, tensor), P(tensor, dp))
    return jax.shard_map(
        on_device, mesh=grid, in_specs=in_specs, out_specs=out_specs, check_vma=False
    )
```

```python
import functools

import jax
import jax.numpy as jnp
from jax import lax
from jax.experimental import pallas as pl
from jax.experimental.pallas import tpu as pltpu
from jax.sharding import PartitionSpec as P

HB = 256
SCALE = 64.0
AXES = ("x", "core", "z", "y")
BF16 = jnp.bfloat16
F32 = jnp.float32
VMEM = pl.BlockSpec(memory_space=pltpu.VMEM)
ANY = pl.BlockSpec(memory_space=pl.ANY)


def move(value, route, turn=0):
    nx, nc, nz, ny = (lax.axis_size(axis) for axis in AXES)

    def flat(x, c, z, y):
        return ((x % nx * nc + c) * nz + z) * ny + y

    pairs = [
        (flat(x, c, z, y), flat(*route(x, c, z, y)))
        for x in range(nx)
        for c in range(nc)
        for z in range(nz)
        for y in range(ny)
    ]
    return lax.ppermute(value, AXES, pairs[turn:] + pairs[:turn])


def swap(value, turn=0):
    return move(value, lambda x, c, z, y: (x, 1 - c, z, y), turn)


def forward(value):
    return move(value, lambda x, c, z, y: (x + 1 - 2 * c, c, z, y))


def backward(value):
    return move(value, lambda x, c, z, y: (x - 1 + 2 * c, c, z, y))


def across(value):
    return move(value, lambda x, c, z, y: (x + 2, c, z, y))


def hadamard(order):
    i = jnp.arange(order, dtype=jnp.int32)
    both = jnp.bitwise_and(i[:, None], i[None, :])
    return (1 - 2 * (lax.population_count(both) % 2)).astype(BF16)


def after(value, *earlier):
    return lax.optimization_barrier((value,) + earlier)[0]


def in_hbm(value):
    return pltpu.with_memory_space_constraint(value, pltpu.HBM)


def call(kernel, name, mib, in_specs, out_specs, out_shape, scratch_shapes=(), grid=()):
    return pl.pallas_call(
        kernel,
        grid=grid,
        in_specs=in_specs,
        out_specs=out_specs,
        out_shape=out_shape,
        scratch_shapes=scratch_shapes,
        compiler_params=pltpu.CompilerParams(vmem_limit_bytes=mib * 2**20),
        cost_estimate=pl.CostEstimate(flops=1, bytes_accessed=1, transcendentals=0),
        name=name,
    )


def split_kernel(grad_ref, kept_ref, given_ref, sems):
    x, core = lax.axis_index("x"), lax.axis_index("core")
    cols = kept_ref.shape[-1]
    opposite, here = lax.rem(x + 2, 4), x
    ahead, back = lax.rem(x + 5 - 2 * core, 4), lax.rem(x + 3 + 2 * core, 4)
    kept = ((opposite, core), (here, core), (ahead, core), (ahead, 1 - core))
    given = ((opposite, 1 - core), (here, 1 - core), (back, 1 - core), (back, core))
    copies = []
    for out, blocks in ((kept_ref, kept), (given_ref, given)):
        for i, (chip, its_core) in enumerate(blocks):
            part = pl.ds(pl.multiple_of((chip * 2 + its_core) * cols, cols), cols)
            copies.append(
                pltpu.make_async_copy(grad_ref.at[:, part], out.at[i], sems.at[len(copies)])
            )
            copies[-1].start()
    for copy in copies:
        copy.wait()


def split(out_grad, cols):
    shape = pltpu.VMEM((4, out_grad.shape[0], cols), BF16)
    return call(
        split_kernel, "split", 4, [ANY], [ANY] * 2, [shape] * 2, [pltpu.SemaphoreType.DMA((8,))]
    )(in_hbm(out_grad))


def pair_kernel(kept_ref, got_ref, opp_ref, own_ref, ahead_ref):
    tokens = kept_ref.shape[1]
    for i, (ref, row) in enumerate(
        ((opp_ref, 0), (own_ref, 0), (ahead_ref, 0), (ahead_ref, 2 * tokens))
    ):
        ref[row : row + tokens, :] = kept_ref[i]
        ref[row + tokens : row + 2 * tokens, :] = got_ref[i]


def pair(kept, got):
    tokens, cols = kept.shape[1:]
    return call(
        pair_kernel,
        "pair",
        4,
        [VMEM, VMEM],
        [VMEM] * 3,
        [pltpu.VMEM((rows * tokens, cols), BF16) for rows in (2, 2, 4)],
    )(kept, got)


def store_rows(value, outs):
    row = 0
    for out in outs:
        out[...] = value[row : row + out.shape[0]]
        row += out.shape[0]


def stream(hbm_ref, held_ref, sems):
    copies = []
    for i in range(hbm_ref.shape[0] // HB):
        part = pl.ds(i * HB, HB)
        copies.append(pltpu.make_async_copy(hbm_ref.at[part, :], held_ref.at[part, :], sems.at[i]))
        copies[-1].start()
    return copies


def streamed(ff, cols):
    return [pltpu.VMEM((ff, cols), BF16), pltpu.SemaphoreType.DMA((ff // HB,))]


def quantize_kernel(table_ref, weight_ref, inv_ref, grad_ref, turned_ref, keep_ref, *refs):
    outs, (held, sems) = refs[:-2], refs[-2:]
    copies = stream(weight_ref, held, sems)
    inv = inv_ref[...]
    step = (1.0 / SCALE) / inv
    for i, copy in enumerate(copies):
        part = pl.ds(i * HB, HB)
        copy.wait()
        raw_code = jnp.floor(held[part, :].astype(F32) * inv + 0.5)
        code = jnp.clip(raw_code, -8.0, 7.0)
        keep_ref[part, :] = jnp.where(raw_code == code, 1.0, 0.0).astype(BF16)
        turned = jnp.dot(table_ref[...], code.astype(BF16), preferred_element_type=F32)
        turned_ref[part, :] = (turned * step).astype(BF16)
        result = lax.dot_general(
            grad_ref[...], turned_ref[part, :], (((1,), (1,)), ((), ())), preferred_element_type=F32
        ).astype(BF16)
        store_rows(result, [out.at[:, part] for out in outs])


def quantize(table, weight, inv, grads, rows):
    ff, cols = weight.shape
    return call(
        quantize_kernel,
        "quantize",
        14,
        [VMEM, ANY, VMEM, VMEM],
        [VMEM] * (2 + len(rows)),
        [pltpu.VMEM((ff, cols), BF16)] * 2 + [pltpu.VMEM((count, ff), BF16) for count in rows],
        streamed(ff, cols),
    )(table, in_hbm(weight), inv, grads)


def product_kernel(count, *refs):
    grads, turned_ref, outs = refs[:count], refs[count], refs[count + 1 :]
    rows = sum(out.shape[0] for out in outs) // count
    for i in range(turned_ref.shape[0] // HB):
        part = pl.ds(i * HB, HB)
        result = lax.dot_general(
            jnp.concatenate([ref[:rows, :] for ref in grads]) if count > 1 else grads[0][:rows, :],
            turned_ref[part, :],
            (((1,), (1,)), ((), ())),
            preferred_element_type=F32,
        ).astype(BF16)
        store_rows(result, [out.at[:, part] for out in outs])


def product(grads, turned, rows):
    ff = turned.shape[0]
    return call(
        functools.partial(product_kernel, len(grads)),
        "product",
        8,
        [VMEM] * (len(grads) + 1),
        [VMEM] * len(rows),
        [pltpu.VMEM((size, ff), BF16) for size in rows],
    )(*grads, turned)


def add_kernel(first_rows, pieces, *refs):
    outs = refs[sum(pieces) :]
    terms, start = [], 0
    for count in pieces:
        terms.append(refs[start : start + count])
        start += count
    height = sum(out.shape[0] for out in outs)
    for i in range(outs[0].shape[1] // HB):
        part = pl.ds(i * HB, HB)
        total = None
        for row, term in zip(first_rows, terms):
            value = [ref[:, part] if len(term) > 1 else ref[row : row + height, part] for ref in term]
            value = value[0] if len(value) == 1 else jnp.concatenate(value)
            value = value.astype(F32)
            total = value if total is None else total + value
        store_rows(total.astype(BF16), [out.at[:, part] for out in outs])


def add(name, rows, *terms):
    first_rows = [term[1] if isinstance(term, tuple) else 0 for term in terms]
    terms = [
        term if isinstance(term, list) else [term[0] if isinstance(term, tuple) else term]
        for term in terms
    ]
    ff = terms[0][0].shape[1]
    flat = [piece for term in terms for piece in term]
    return call(
        functools.partial(add_kernel, tuple(first_rows), tuple(len(term) for term in terms)),
        name,
        6,
        [VMEM] * len(flat),
        [VMEM] * len(rows),
        [pltpu.VMEM((count, ff), BF16) for count in rows],
    )(*flat)


def my_sign(step):
    core, z, y = (lax.axis_index(axis) for axis in ("core", "z", "y"))
    bit, y_first = mix_axis(step)
    place = jnp.where((core == 0) == y_first, y, z)
    return jnp.where(jnp.bitwise_and(place, bit) == 0, 1.0, -1.0).astype(F32)


def mix_kernel(step, *refs):
    sign = my_sign(step)
    half = len(refs) // 2
    values, partners, out_ref = refs[:half], refs[half:-1], refs[-1]
    row = 0
    for value_ref, partner_ref in zip(values, partners):
        rows = pl.ds(row, value_ref.shape[0])
        row += value_ref.shape[0]
        for i in range(value_ref.shape[1] // HB):
            part = pl.ds(i * HB, HB)
            total = value_ref[:, part].astype(F32) * sign + partner_ref[:, part].astype(F32)
            out_ref[rows, part] = total.astype(BF16)


def mix(name, step, values, partners, last=False):
    shape = (sum(value.shape[0] for value in values), values[0].shape[1])
    return call(
        functools.partial(mix_kernel, step),
        name,
        6,
        [VMEM] * (2 * len(values)),
        VMEM,
        jax.ShapeDtypeStruct(shape, BF16) if last else pltpu.VMEM(shape, BF16),
    )(*values, *partners)


def rotate_kernel(step, table_ref, value_ref, partner_ref, rotated_ref):
    sign = my_sign(step)
    for i in range(value_ref.shape[1] // HB):
        part = pl.ds(i * HB, HB)
        mix = value_ref[:, part].astype(F32) * sign + partner_ref[:, part].astype(F32)
        turned = lax.dot_general(
            table_ref[...], mix.astype(BF16), (((1,), (1,)), ((), ())), preferred_element_type=F32
        )
        rotated_ref[part, :] = (turned * (1.0 / SCALE)).astype(BF16)


def rotate(table, step, value, partner):
    tokens, ff = value.shape
    return call(
        functools.partial(rotate_kernel, step),
        "rotate",
        8,
        [VMEM] * 3,
        VMEM,
        pltpu.VMEM((ff, tokens), BF16),
    )(table, value, partner)


def partial_sum(rotated, grads, part):
    left = jnp.concatenate([ref[part, :] for ref in rotated], axis=1)
    return jnp.dot(left, grads, preferred_element_type=F32)


def early_kernel(count, pieces, *refs):
    rotated, grads = refs[:count], refs[count:-2]
    out_ref, all_grads = refs[-2:]
    tokens = rotated[0].shape[1]
    row = 0
    for ref, piece in zip(grads, pieces):
        rows = 2 * tokens // piece
        all_grads[pl.ds(row, rows), :] = ref[:rows, :]
        row += rows
    for i in range(out_ref.shape[0] // HB):
        part = pl.ds(i * HB, HB)
        out_ref[part, :] = partial_sum(rotated, all_grads[...], part)


def early_product(rotated, grads):
    count = len(rotated)
    flat = [piece for chip in grads for piece in chip]
    pieces = tuple(len(chip) for chip in grads for _ in chip)
    ff, cols = rotated[0].shape[0], flat[0].shape[1]
    return call(
        functools.partial(early_kernel, count, pieces),
        "early_product",
        10,
        [VMEM] * (count + len(flat)),
        VMEM,
        pltpu.VMEM((ff, cols), F32),
        [pltpu.VMEM((count * rotated[0].shape[1], cols), BF16)],
    )(*rotated, *flat)


def late_kernel(mine_ref, other_ref, grad_ref, keep_ref, early_ref, out_ref, held, sems):
    copies = []
    for i in range(early_ref.shape[0] // HB):
        part = pl.ds(i * HB, HB)
        total = early_ref[part, :] + partial_sum((mine_ref, other_ref), grad_ref[...], part)
        held[part, :] = jnp.where(keep_ref[part, :].astype(F32) > 0.0, total, 0.0).astype(BF16)
        copies.append(pltpu.make_async_copy(held.at[part, :], out_ref.at[part, :], sems.at[i]))
        copies[-1].start()
    for copy in copies:
        copy.wait()


def late_product(mine, other, grads, keep, early):
    return call(
        late_kernel,
        "late_product",
        14,
        [VMEM] * 5,
        ANY,
        jax.ShapeDtypeStruct(early.shape, BF16),
        streamed(*early.shape),
    )(mine, other, grads, keep, early)


def mix_axis(step):
    return 1 << (step % 2), step < 2


def partner(value, step):
    bit, y_first = mix_axis(step)

    def route(x, c, z, y):
        return (x, c, z, y ^ bit) if (c == 0) == y_first else (x, c, z ^ bit, y)

    return move(value, route)


def on_device(hidden, out_grad, weight, inv_scale):
    table = hadamard(HB)
    inv = inv_scale[None, :]
    tokens = hidden.shape[0]
    half = tokens // 2
    whole, halves = (tokens,), (half, half)

    kept, given = split(after(out_grad, table), weight.shape[1])
    got = partner(hidden, 0)
    to_opp, own, to_ahead = pair(kept, swap(given))
    opp, bwd = across(to_opp), forward(to_ahead)
    turned, keep, own_mine, own_other = quantize(table, weight, inv, own, whole * 2)
    own_other = swap(own_other, 1)

    hid = mix("mix", 0, [after(hidden, turned)], [got])
    got = partner(hid, 1)
    bwd = after(bwd, hid)
    fwd = [swap(bwd[(2 + j) * tokens : (3 + j) * tokens], 2 + j) for j in (0, 1)]
    bwd_parts = product([bwd], turned, halves * 2)
    bwd_mine = [swap(bwd_parts[j], 4 + j) for j in (0, 1)]
    bwd_other = [swap(bwd_parts[2 + j], 6 + j) for j in (0, 1)]
    fwd_other, *fwd_mine = product([after(fwd[0], bwd_parts[0]), fwd[1]], turned, whole + halves)
    opp_mine, *opp_other = product([after(opp, fwd_other)], turned, whole + halves)
    opp_other = [swap(opp_other[j], 8 + j) for j in (0, 1)]
    own_sum = add("add_own", halves, after(own_mine, opp_mine), own_other)
    (second_send,) = add("add_second", whole, after(fwd_other, own_sum[0]), bwd_mine)
    second = forward(second_send)
    first = []
    last = second_send
    for j in (0, 1):
        (last,) = add("add_first", (half,), (after(opp_mine, last), j * half), opp_other[j])
        first.append(forward(last))
    hid = mix("mix", 1, [after(hid, last)], [got])
    got = partner(hid, 2)
    second = after(second, hid)
    second_other = swap(second, 10)
    third = []
    last = second
    for j in (0, 1):
        (last,) = add("add_third", (half,), after(first[j], last), fwd_mine[j], bwd_other[j])
        third.append(forward(last))
    hid = mix("mix", 2, [after(hid, last)], [got])
    got = partner(hid, 3)
    last = hid

    values, partners = [], []
    for j in (0, 1):
        (last,) = add(
            "add_grad", (half,), own_sum[j], (second_other, j * half), after(third[j], last)
        )
        values.append(last)
        partners.append(partner(last, 0))
        if j == 0:
            last = rotated = rotate(table, 3, after(hid, last), got)
            bwd_a, fwd_a = forward(rotated), backward(rotated)
            other = swap(rotated, 11)
    for step in range(3):
        for j in (0, 1):
            last = mix("mix_grad", step, [after(values[j], last)], [partners[j]])
            values[j] = last
            partners[j] = partner(last, step + 1)
        if step == 0:
            bwd_a = after(bwd_a, last)
            opp_a = forward(bwd_a)
            fwd_b = swap(bwd_a, 12)
        if step == 1:
            fwd_a = after(fwd_a, last)
            bwd_b = swap(fwd_a, 13)
            last = early = early_product(
                [rotated, other, bwd_a, bwd_b, fwd_b, fwd_a], [[own], [bwd], fwd]
            )
    opp_a = after(opp_a, last)
    weight_grad = late_product(opp_a, swap(opp_a, 14), opp, keep, early)
    hidden_grad = mix("mix_last", 3, [after(values[0], weight_grad), values[1]], partners, last=True)
    return hidden_grad, weight_grad


def solution(mesh):
    grid = jax.sharding.Mesh(mesh.devices.reshape(4, 2, 4, 4), AXES)
    dp, tensor = ("x", "core"), ("z", "y")
    in_specs = (P(dp, tensor), P(dp, None), P(tensor, dp), P(dp))
    out_specs = (P(dp, tensor), P(tensor, dp))
    return jax.shard_map(
        on_device, mesh=grid, in_specs=in_specs, out_specs=out_specs, check_vma=False
    )
```

```python
import functools

import jax
import jax.numpy as jnp
from jax import lax
from jax.experimental import pallas as pl
from jax.experimental.pallas import tpu as pltpu
from jax.sharding import PartitionSpec as P

HB = 256
SCALE = 64.0
BEHIND = (0, 2, 1, 3)
AXES = ("x", "core", "z", "y")
BF16 = jnp.bfloat16
F32 = jnp.float32
VMEM = pl.BlockSpec(memory_space=pltpu.VMEM)
ANY = pl.BlockSpec(memory_space=pl.ANY)


def move(value, route, turn=0):
    nx, nc, nz, ny = (lax.axis_size(axis) for axis in AXES)

    def flat(x, c, z, y):
        return ((x % nx * nc + c) * nz + z) * ny + y

    pairs = [
        (flat(x, c, z, y), flat(*route(x, c, z, y)))
        for x in range(nx)
        for c in range(nc)
        for z in range(nz)
        for y in range(ny)
    ]
    return lax.ppermute(value, AXES, pairs[turn:] + pairs[:turn])


def swap(value, turn=0):
    return move(value, lambda x, c, z, y: (x, 1 - c, z, y), turn)


def forward(value):
    return move(value, lambda x, c, z, y: (x + 1 - 2 * c, c, z, y))


def backward(value):
    return move(value, lambda x, c, z, y: (x - 1 + 2 * c, c, z, y))


def forward_crossed(value):
    return move(value, lambda x, c, z, y: (x + 1 - 2 * c, 1 - c, z, y))


def across(value):
    return move(value, lambda x, c, z, y: (x + 2, c, z, y))


def hadamard(order):
    i = jnp.arange(order, dtype=jnp.int32)
    both = jnp.bitwise_and(i[:, None], i[None, :])
    return (1 - 2 * (lax.population_count(both) % 2)).astype(BF16)


def after(value, *earlier):
    return lax.optimization_barrier((value,) + earlier)[0]


def in_hbm(value):
    return pltpu.with_memory_space_constraint(value, pltpu.HBM)


def call(kernel, name, mib, in_specs, out_specs, out_shape, scratch_shapes=(), grid=(), flops=1):
    return pl.pallas_call(
        kernel,
        grid=grid,
        in_specs=in_specs,
        out_specs=out_specs,
        out_shape=out_shape,
        scratch_shapes=scratch_shapes,
        compiler_params=pltpu.CompilerParams(vmem_limit_bytes=mib * 2**20),
        cost_estimate=pl.CostEstimate(flops=flops, bytes_accessed=1, transcendentals=0),
        name=name,
    )


def split_kernel(grad_ref, kept_ref, given_ref, sems):
    x, core = lax.axis_index("x"), lax.axis_index("core")
    cols = kept_ref.shape[-1]
    opposite, here = lax.rem(x + 2, 4), x
    ahead, back = lax.rem(x + 5 - 2 * core, 4), lax.rem(x + 3 + 2 * core, 4)
    kept = ((opposite, core), (here, core), (ahead, core), (ahead, 1 - core))
    given = ((opposite, 1 - core), (here, 1 - core), (back, 1 - core), (back, core))
    copies = []
    for out, blocks in ((kept_ref, kept), (given_ref, given)):
        for i, (chip, its_core) in enumerate(blocks):
            part = pl.ds(pl.multiple_of((chip * 2 + its_core) * cols, cols), cols)
            copies.append(
                pltpu.make_async_copy(grad_ref.at[:, part], out.at[i], sems.at[len(copies)])
            )
            copies[-1].start()
    for copy in copies:
        copy.wait()


def split(out_grad, cols):
    shape = pltpu.VMEM((4, out_grad.shape[0], cols), BF16)
    return call(
        split_kernel, "split", 4, [ANY], [ANY] * 2, [shape] * 2, [pltpu.SemaphoreType.DMA((8,))]
    )(in_hbm(out_grad))


def pair_kernel(kept_ref, got_ref, opp_ref, own_ref, ahead_ref):
    tokens = kept_ref.shape[1]
    for i, (ref, row) in enumerate(
        ((opp_ref, 0), (own_ref, 0), (ahead_ref, 0), (ahead_ref, 2 * tokens))
    ):
        ref[row : row + tokens, :] = kept_ref[i]
        ref[row + tokens : row + 2 * tokens, :] = got_ref[i]


def pair(kept, got):
    tokens, cols = kept.shape[1:]
    return call(
        pair_kernel,
        "pair",
        4,
        [VMEM, VMEM],
        [VMEM] * 3,
        [pltpu.VMEM((rows * tokens, cols), BF16) for rows in (2, 2, 4)],
    )(kept, got)


def store_rows(value, outs):
    row = 0
    for out in outs:
        out[...] = value[row : row + out.shape[0]]
        row += out.shape[0]


def stream(hbm_ref, held_ref, sems):
    copies = []
    for i in range(hbm_ref.shape[0] // HB):
        part = pl.ds(i * HB, HB)
        copies.append(pltpu.make_async_copy(hbm_ref.at[part, :], held_ref.at[part, :], sems.at[i]))
        copies[-1].start()
    return copies


def streamed(ff, cols):
    return [pltpu.VMEM((ff, cols), BF16), pltpu.SemaphoreType.DMA((ff // HB,))]


def quantize_kernel(table_ref, weight_ref, inv_ref, grad_ref, turned_ref, keep_ref, *refs):
    outs, (held, sems) = refs[:-2], refs[-2:]
    copies = stream(weight_ref, held, sems)
    inv = inv_ref[...]
    step = (1.0 / SCALE) / inv
    for i, copy in enumerate(copies):
        part = pl.ds(i * HB, HB)
        copy.wait()
        raw_code = jnp.floor(held[part, :].astype(F32) * inv + 0.5)
        code = jnp.clip(raw_code, -8.0, 7.0)
        keep_ref[part, :] = jnp.where(raw_code == code, 1.0, 0.0).astype(BF16)
        turned = jnp.dot(table_ref[...], code.astype(BF16), preferred_element_type=F32)
        turned_ref[part, :] = (turned * step).astype(BF16)
        result = lax.dot_general(
            grad_ref[...], turned_ref[part, :], (((1,), (1,)), ((), ())), preferred_element_type=F32
        ).astype(BF16)
        store_rows(result, [out.at[:, part] for out in outs])


def quantize(table, weight, inv, grads, rows):
    ff, cols = weight.shape
    return call(
        quantize_kernel,
        "quantize",
        14,
        [VMEM, ANY, VMEM, VMEM],
        [VMEM] * (2 + len(rows)),
        [pltpu.VMEM((ff, cols), BF16)] * 2 + [pltpu.VMEM((count, ff), BF16) for count in rows],
        streamed(ff, cols),
    )(table, in_hbm(weight), inv, grads)


def product_kernel(count, *refs):
    grads, turned_ref, outs = refs[:count], refs[count], refs[count + 1 :]
    rows = sum(out.shape[0] for out in outs) // count
    for i in range(turned_ref.shape[0] // HB):
        part = pl.ds(i * HB, HB)
        result = lax.dot_general(
            jnp.concatenate([ref[:rows, :] for ref in grads]) if count > 1 else grads[0][:rows, :],
            turned_ref[part, :],
            (((1,), (1,)), ((), ())),
            preferred_element_type=F32,
        ).astype(BF16)
        store_rows(result, [out.at[:, part] for out in outs])


def product(grads, turned, rows, flops=1):
    ff = turned.shape[0]
    return call(
        functools.partial(product_kernel, len(grads)),
        "product",
        8,
        [VMEM] * (len(grads) + 1),
        [VMEM] * len(rows),
        [pltpu.VMEM((size, ff), BF16) for size in rows],
        flops=flops,
    )(*grads, turned)


def add_kernel(first_rows, pieces, *refs):
    outs = refs[sum(pieces) :]
    terms, start = [], 0
    for count in pieces:
        terms.append(refs[start : start + count])
        start += count
    height = sum(out.shape[0] for out in outs)
    for i in range(outs[0].shape[1] // HB):
        part = pl.ds(i * HB, HB)
        total = None
        for row, term in zip(first_rows, terms):
            value = [ref[:, part] if len(term) > 1 else ref[row : row + height, part] for ref in term]
            value = value[0] if len(value) == 1 else jnp.concatenate(value)
            value = value.astype(F32)
            total = value if total is None else total + value
        store_rows(total.astype(BF16), [out.at[:, part] for out in outs])


def add(name, rows, *terms):
    first_rows = [term[1] if isinstance(term, tuple) else 0 for term in terms]
    terms = [
        term if isinstance(term, list) else [term[0] if isinstance(term, tuple) else term]
        for term in terms
    ]
    ff = terms[0][0].shape[1]
    flat = [piece for term in terms for piece in term]
    return call(
        functools.partial(add_kernel, tuple(first_rows), tuple(len(term) for term in terms)),
        name,
        6,
        [VMEM] * len(flat),
        [VMEM] * len(rows),
        [pltpu.VMEM((count, ff), BF16) for count in rows],
    )(*flat)


def my_sign(step):
    core, z, y = (lax.axis_index(axis) for axis in ("core", "z", "y"))
    bit, y_first = mix_axis(step)
    place = jnp.where((core == 0) == y_first, y, z)
    return jnp.where(jnp.bitwise_and(place, bit) == 0, 1.0, -1.0).astype(F32)


def mix_kernel(step, *refs):
    sign = my_sign(step)
    half = len(refs) // 2
    values, partners, out_ref = refs[:half], refs[half:-1], refs[-1]
    row = 0
    for value_ref, partner_ref in zip(values, partners):
        rows = pl.ds(row, value_ref.shape[0])
        row += value_ref.shape[0]
        for i in range(value_ref.shape[1] // HB):
            part = pl.ds(i * HB, HB)
            total = value_ref[:, part].astype(F32) * sign + partner_ref[:, part].astype(F32)
            out_ref[rows, part] = total.astype(BF16)


def mix(name, step, values, partners, last=False):
    shape = (sum(value.shape[0] for value in values), values[0].shape[1])
    return call(
        functools.partial(mix_kernel, step),
        name,
        6,
        [VMEM] * (2 * len(values)),
        VMEM,
        jax.ShapeDtypeStruct(shape, BF16) if last else pltpu.VMEM(shape, BF16),
    )(*values, *partners)


def rotate_kernel(step, table_ref, value_ref, partner_ref, rotated_ref):
    sign = my_sign(step)
    for i in range(value_ref.shape[1] // HB):
        part = pl.ds(i * HB, HB)
        mix = value_ref[:, part].astype(F32) * sign + partner_ref[:, part].astype(F32)
        turned = lax.dot_general(
            table_ref[...], mix.astype(BF16), (((1,), (1,)), ((), ())), preferred_element_type=F32
        )
        rotated_ref[part, :] = (turned * (1.0 / SCALE)).astype(BF16)


def rotate(table, step, value, partner):
    tokens, ff = value.shape
    return call(
        functools.partial(rotate_kernel, step),
        "rotate",
        8,
        [VMEM] * 3,
        VMEM,
        pltpu.VMEM((ff, tokens), BF16),
    )(table, value, partner)


def partial_sum(rotated, grads, part):
    left = jnp.concatenate([ref[part, :] for ref in rotated], axis=1)
    return jnp.dot(left, grads, preferred_element_type=F32)


def gather_rows(blocks, refs, all_grads):
    tokens = all_grads.shape[0] // len(blocks)
    for i, (which, row) in enumerate(blocks):
        all_grads[pl.ds(i * tokens, tokens), :] = refs[which][row * tokens : (row + 1) * tokens, :]


def early_kernel(blocks, *refs):
    count = len(blocks)
    rotated, grads, (out_ref, all_grads) = refs[:count], refs[count:-2], refs[-2:]
    gather_rows(blocks, grads, all_grads)
    for i in range(out_ref.shape[0] // HB):
        part = pl.ds(i * HB, HB)
        out_ref[part, :] = partial_sum(rotated, all_grads[...], part)


def early_product(rotated, blocks, grads):
    ff, tokens = rotated[0].shape
    cols = grads[0].shape[1]
    return call(
        functools.partial(early_kernel, blocks),
        "early_product",
        10,
        [VMEM] * (len(rotated) + len(grads)),
        VMEM,
        pltpu.VMEM((ff, cols), F32),
        [pltpu.VMEM((len(rotated) * tokens, cols), BF16)],
    )(*rotated, *grads)


def late_kernel(blocks, *refs):
    count = len(blocks)
    rotated, grads = refs[:count], refs[count:-6]
    keep_ref, early_ref, out_ref, all_grads, held, sems = refs[-6:]
    gather_rows(blocks, grads, all_grads)
    copies = []
    for i in range(early_ref.shape[0] // HB):
        part = pl.ds(i * HB, HB)
        total = early_ref[part, :] + partial_sum(rotated, all_grads[...], part)
        held[part, :] = jnp.where(keep_ref[part, :].astype(F32) > 0.0, total, 0.0).astype(BF16)
        copies.append(pltpu.make_async_copy(held.at[part, :], out_ref.at[part, :], sems.at[i]))
        copies[-1].start()
    for copy in copies:
        copy.wait()


def late_product(rotated, blocks, grads, keep, early):
    tokens = rotated[0].shape[1]
    return call(
        functools.partial(late_kernel, blocks),
        "late_product",
        14,
        [VMEM] * (len(rotated) + len(grads) + 2),
        ANY,
        jax.ShapeDtypeStruct(early.shape, BF16),
        [pltpu.VMEM((len(rotated) * tokens, early.shape[1]), BF16)] + streamed(*early.shape),
    )(*rotated, *grads, keep, early)


def place(stage):
    core, z, y = (lax.axis_index(axis) for axis in ("core", "z", "y"))
    return jnp.where((core == 0) == (stage == 0), y, z)


def quarter(index, rows):
    return pl.ds(pl.multiple_of(jnp.bitwise_and(index, 3) * rows, rows), rows)


def deal_kernel(stage, *refs):
    terms, outs = refs[:-4], refs[-4:]
    mine = place(stage)
    rows = outs[0].shape[0]
    for k, out in enumerate(outs):
        part_rows = quarter(mine + k, rows)
        for i in range(out.shape[1] // HB):
            part = pl.ds(i * HB, HB)
            out[:, part] = sum(ref[part_rows, part].astype(F32) for ref in terms).astype(BF16)


def deal(name, stage, *terms):
    tokens, ff = terms[0].shape
    return call(
        functools.partial(deal_kernel, stage),
        name,
        6,
        [VMEM] * len(terms),
        [VMEM] * 4,
        [pltpu.VMEM((tokens // 4, ff), BF16)] * 4,
    )(*terms)


def spread(pieces, stage):
    def route(distance):
        def to(x, c, z, y):
            if (c == 0) == (stage == 0):
                return (x, c, z, (y + distance) % 4)
            return (x, c, (z + distance) % 4, y)

        return to

    return [pieces[0]] + [move(pieces[k], route(k)) for k in BEHIND[1:]]


def mix_quarters_kernel(stage, *refs):
    values, outs = refs[:4], refs[4:]
    mine = place(stage)
    for k, out in enumerate(outs):
        signs = []
        for m in BEHIND:
            both = jnp.bitwise_and(jnp.bitwise_and(mine + k, mine - m), 3)
            odd = jnp.bitwise_and(both + (both >> 1), 1)
            signs.append((1 - 2 * odd).astype(F32))
        for i in range(out.shape[1] // HB):
            part = pl.ds(i * HB, HB)
            total = sum(ref[:, part].astype(F32) * sign for ref, sign in zip(values, signs))
            out[:, part] = total.astype(BF16)


def mix_quarters(stage, values):
    return call(
        functools.partial(mix_quarters_kernel, stage),
        "mix_quarters",
        6,
        [VMEM] * 4,
        [VMEM] * 4,
        [pltpu.VMEM(values[0].shape, BF16)] * 4,
    )(*values)


def collect_kernel(*refs):
    values, outs = refs[:4], refs[4:]
    rows = values[0].shape[0]
    if len(outs) == 1:
        for k, ref in zip(BEHIND, values):
            outs[0][quarter(place(1) - k, rows), :] = ref[...]
        return
    outs, held = outs[:4], outs[4]
    for k, ref in zip(BEHIND, values):
        held[quarter(place(0) - k, rows), :] = ref[...]
    for k, out in enumerate(outs):
        out[...] = held[quarter(place(1) + k, rows), :]


def collect(values, last):
    rows, ff = values[0].shape
    whole = (4 * rows, ff)
    return call(
        collect_kernel,
        "collect",
        6,
        [VMEM] * 4,
        VMEM if last else [VMEM] * 4,
        jax.ShapeDtypeStruct(whole, BF16) if last else [pltpu.VMEM((rows, ff), BF16)] * 4,
        [] if last else [pltpu.VMEM(whole, BF16)],
    )(*values)


def mix_axis(step):
    return 1 << (step // 2), step % 2 == 0


def partner(value, step):
    bit, y_first = mix_axis(step)

    def route(x, c, z, y):
        return (x, c, z, y ^ bit) if (c == 0) == y_first else (x, c, z ^ bit, y)

    return move(value, route)


def on_device(hidden, out_grad, weight, inv_scale):
    table = hadamard(HB)
    inv = inv_scale[None, :]
    tokens = hidden.shape[0]
    half = tokens // 2
    whole, halves = (tokens,), (half, half)

    kept, given = split(after(out_grad, table), weight.shape[1])
    got = partner(hidden, 0)
    to_opp, own, to_ahead = pair(kept, swap(given))
    opp, bwd = across(to_opp), forward(to_ahead)
    turned, keep, own_mine, own_other = quantize(table, weight, inv, own, whole * 2)
    own_other = swap(own_other, 1)

    hid = mix("mix", 0, [after(hidden, turned)], [got])
    got = partner(hid, 1)
    opp_mine, *opp_other = product([after(opp, hid)], turned, whole + halves)
    opp_other = [swap(opp_other[j], 8 + j) for j in (0, 1)]
    (first_send,) = add("add_first", whole, opp_mine, opp_other)
    first = forward(first_send)
    bwd = after(bwd, first_send)
    fwd = [swap(bwd[(2 + j) * tokens : (3 + j) * tokens], 2 + j) for j in (0, 1)]
    bwd_parts = product([bwd], turned, halves * 2)
    bwd_mine = [swap(bwd_parts[j], 4 + j) for j in (0, 1)]
    bwd_other = [swap(bwd_parts[2 + j], 6 + j) for j in (0, 1)]
    hid = mix("mix", 1, [after(hid, bwd_parts[0])], [got])
    got = partner(hid, 2)
    (own_sum,) = add("add_own", whole, after(own_mine, hid), own_other)
    fwd_other, *fwd_mine = product(
        [after(fwd[0], own_sum, first), fwd[1]], turned, whole + halves
    )
    (third_send,) = add("add_third", whole, after(first, fwd_other), list(fwd_mine), bwd_other)
    third = forward(third_send)
    (second_send,) = add("add_second", whole, after(fwd_other, third_send), bwd_mine)
    second = forward_crossed(second_send)
    hid = mix("mix", 2, [after(hid, second_send)], [got])
    got = partner(hid, 3)

    pieces = deal("deal_grad", 0, own_sum, after(second, hid), after(third, hid))
    values = spread(pieces, 0)
    rotated = rotate(table, 3, after(hid, pieces[0]), got)
    bwd_a, fwd_a = forward(rotated), backward(rotated)
    other = swap(rotated, 11)
    pieces = mix_quarters(0, [after(values[0], rotated)] + values[1:])
    values = spread(pieces, 0)
    pieces = collect([after(values[0], bwd_a, fwd_a)] + values[1:], False)
    opp_a = forward(bwd_a)
    fwd_b, bwd_b = swap(after(bwd_a, pieces[0]), 12), swap(after(fwd_a, pieces[0]), 13)
    values = spread(pieces, 1)
    early = early_product(
        [rotated, other, bwd_a, bwd_b, fwd_b, fwd_a],
        ((0, 0), (0, 1), (1, 0), (1, 1), (2, 0), (3, 0)),
        [own, bwd] + fwd,
    )
    pieces = mix_quarters(1, [after(values[0], early)] + values[1:])
    values = spread(pieces, 1)
    opp_a = after(opp_a, pieces[0])
    weight_grad = late_product(
        [opp_a, swap(opp_a, 14)], ((0, 0), (0, 1)), [opp], keep, early
    )
    hidden_grad = collect([after(values[0], weight_grad)] + values[1:], True)
    return hidden_grad, weight_grad


def solution(mesh):
    grid = jax.sharding.Mesh(mesh.devices.reshape(4, 2, 4, 4), AXES)
    dp, tensor = ("x", "core"), ("z", "y")
    in_specs = (P(dp, tensor), P(dp, None), P(tensor, dp), P(dp))
    out_specs = (P(dp, tensor), P(tensor, dp))
    return jax.shard_map(
        on_device, mesh=grid, in_specs=in_specs, out_specs=out_specs, check_vma=False
    )
```

```python
import functools

import jax
import jax.numpy as jnp
from jax import lax
from jax.experimental import pallas as pl
from jax.experimental.pallas import tpu as pltpu
from jax.sharding import PartitionSpec as P

HB = 256
SCALE = 64.0
THIRD_FLOPS = 2 * 10**9
BEHIND = (0, 2, 1, 3)
AXES = ("x", "core", "z", "y")
BF16 = jnp.bfloat16
F32 = jnp.float32
VMEM = pl.BlockSpec(memory_space=pltpu.VMEM)
ANY = pl.BlockSpec(memory_space=pl.ANY)


def move(value, route, turn=0):
    nx, nc, nz, ny = (lax.axis_size(axis) for axis in AXES)

    def flat(x, c, z, y):
        return ((x % nx * nc + c) * nz + z) * ny + y

    pairs = [
        (flat(x, c, z, y), flat(*route(x, c, z, y)))
        for x in range(nx)
        for c in range(nc)
        for z in range(nz)
        for y in range(ny)
    ]
    return lax.ppermute(value, AXES, pairs[turn:] + pairs[:turn])


def swap(value, turn=0):
    return move(value, lambda x, c, z, y: (x, 1 - c, z, y), turn)


def forward(value):
    return move(value, lambda x, c, z, y: (x + 1 - 2 * c, c, z, y))


def backward(value):
    return move(value, lambda x, c, z, y: (x - 1 + 2 * c, c, z, y))


def forward_crossed(value):
    return move(value, lambda x, c, z, y: (x + 1 - 2 * c, 1 - c, z, y))


def across(value):
    return move(value, lambda x, c, z, y: (x + 2, c, z, y))


def hadamard(order):
    i = jnp.arange(order, dtype=jnp.int32)
    both = jnp.bitwise_and(i[:, None], i[None, :])
    return (1 - 2 * (lax.population_count(both) % 2)).astype(BF16)


def after(value, *earlier):
    return lax.optimization_barrier((value,) + earlier)[0]


def in_hbm(value):
    return pltpu.with_memory_space_constraint(value, pltpu.HBM)


def call(kernel, name, mib, in_specs, out_specs, out_shape, scratch_shapes=(), grid=(), flops=1):
    return pl.pallas_call(
        kernel,
        grid=grid,
        in_specs=in_specs,
        out_specs=out_specs,
        out_shape=out_shape,
        scratch_shapes=scratch_shapes,
        compiler_params=pltpu.CompilerParams(vmem_limit_bytes=mib * 2**20),
        cost_estimate=pl.CostEstimate(flops=flops, bytes_accessed=1, transcendentals=0),
        name=name,
    )


def split_kernel(grad_ref, kept_ref, given_ref, sems):
    x, core = lax.axis_index("x"), lax.axis_index("core")
    cols = kept_ref.shape[-1]
    opposite, here = lax.rem(x + 2, 4), x
    ahead, back = lax.rem(x + 5 - 2 * core, 4), lax.rem(x + 3 + 2 * core, 4)
    kept = ((opposite, core), (here, core), (ahead, core), (ahead, 1 - core))
    given = ((opposite, 1 - core), (here, 1 - core), (back, 1 - core), (back, core))
    copies = []
    for out, blocks in ((kept_ref, kept), (given_ref, given)):
        for i, (chip, its_core) in enumerate(blocks):
            part = pl.ds(pl.multiple_of((chip * 2 + its_core) * cols, cols), cols)
            copies.append(
                pltpu.make_async_copy(grad_ref.at[:, part], out.at[i], sems.at[len(copies)])
            )
            copies[-1].start()
    for copy in copies:
        copy.wait()


def split(out_grad, cols):
    shape = pltpu.VMEM((4, out_grad.shape[0], cols), BF16)
    return call(
        split_kernel, "split", 4, [ANY], [ANY] * 2, [shape] * 2, [pltpu.SemaphoreType.DMA((8,))]
    )(in_hbm(out_grad))


def pair_kernel(kept_ref, got_ref, opp_ref, own_ref, ahead_ref):
    tokens = kept_ref.shape[1]
    for i, (ref, row) in enumerate(
        ((opp_ref, 0), (own_ref, 0), (ahead_ref, 0), (ahead_ref, 2 * tokens))
    ):
        ref[row : row + tokens, :] = kept_ref[i]
        ref[row + tokens : row + 2 * tokens, :] = got_ref[i]


def pair(kept, got):
    tokens, cols = kept.shape[1:]
    return call(
        pair_kernel,
        "pair",
        4,
        [VMEM, VMEM],
        [VMEM] * 3,
        [pltpu.VMEM((rows * tokens, cols), BF16) for rows in (2, 2, 4)],
    )(kept, got)


def store_rows(value, outs):
    row = 0
    for out in outs:
        out[...] = value[row : row + out.shape[0]]
        row += out.shape[0]


def stream(hbm_ref, held_ref, sems):
    copies = []
    for i in range(hbm_ref.shape[0] // HB):
        part = pl.ds(i * HB, HB)
        copies.append(pltpu.make_async_copy(hbm_ref.at[part, :], held_ref.at[part, :], sems.at[i]))
        copies[-1].start()
    return copies


def streamed(ff, cols):
    return [pltpu.VMEM((ff, cols), BF16), pltpu.SemaphoreType.DMA((ff // HB,))]


def quantize_kernel(table_ref, weight_ref, inv_ref, turned_ref, keep_ref, held, sems):
    copies = stream(weight_ref, held, sems)
    inv = inv_ref[...]
    step = (1.0 / SCALE) / inv
    for i, copy in enumerate(copies):
        part = pl.ds(i * HB, HB)
        copy.wait()
        raw_code = jnp.floor(held[part, :].astype(F32) * inv + 0.5)
        code = jnp.clip(raw_code, -8.0, 7.0)
        keep_ref[part, :] = jnp.where(raw_code == code, 1.0, 0.0).astype(BF16)
        turned = jnp.dot(table_ref[...], code.astype(BF16), preferred_element_type=F32)
        turned_ref[part, :] = (turned * step).astype(BF16)


def quantize(table, weight, inv):
    ff, cols = weight.shape
    return call(
        quantize_kernel,
        "quantize",
        14,
        [VMEM, ANY, VMEM],
        [VMEM] * 2,
        [pltpu.VMEM((ff, cols), BF16)] * 2,
        streamed(ff, cols),
    )(table, in_hbm(weight), inv)


def product_kernel(takes, *refs):
    grads, turned_ref, outs = refs[: len(takes)], refs[len(takes)], refs[len(takes) + 1 :]
    left = [ref[:rows, :] for ref, rows in zip(grads, takes)]
    left = left[0] if len(left) == 1 else jnp.concatenate(left)
    for i in range(turned_ref.shape[0] // HB):
        part = pl.ds(i * HB, HB)
        result = lax.dot_general(
            left, turned_ref[part, :], (((1,), (1,)), ((), ())), preferred_element_type=F32
        ).astype(BF16)
        store_rows(result, [out.at[:, part] for out in outs])


def product(grads, takes, turned, rows):
    ff = turned.shape[0]
    return call(
        functools.partial(product_kernel, takes),
        "product",
        10,
        [VMEM] * (len(grads) + 1),
        [VMEM] * len(rows),
        [pltpu.VMEM((size, ff), BF16) for size in rows],
    )(*grads, turned)


def add_kernel(first_rows, pieces, *refs):
    outs = refs[sum(pieces) :]
    terms, start = [], 0
    for count in pieces:
        terms.append(refs[start : start + count])
        start += count
    height = sum(out.shape[0] for out in outs)
    for i in range(outs[0].shape[1] // HB):
        part = pl.ds(i * HB, HB)
        total = None
        for row, term in zip(first_rows, terms):
            value = [ref[:, part] if len(term) > 1 else ref[row : row + height, part] for ref in term]
            value = value[0] if len(value) == 1 else jnp.concatenate(value)
            value = value.astype(F32)
            total = value if total is None else total + value
        store_rows(total.astype(BF16), [out.at[:, part] for out in outs])


def add(name, rows, *terms, flops=1):
    first_rows = [term[1] if isinstance(term, tuple) else 0 for term in terms]
    terms = [
        term if isinstance(term, list) else [term[0] if isinstance(term, tuple) else term]
        for term in terms
    ]
    ff = terms[0][0].shape[1]
    flat = [piece for term in terms for piece in term]
    return call(
        functools.partial(add_kernel, tuple(first_rows), tuple(len(term) for term in terms)),
        name,
        6,
        [VMEM] * len(flat),
        [VMEM] * len(rows),
        [pltpu.VMEM((count, ff), BF16) for count in rows],
        flops=flops,
    )(*flat)


def my_sign(step):
    core, z, y = (lax.axis_index(axis) for axis in ("core", "z", "y"))
    bit, y_first = mix_axis(step)
    place = jnp.where((core == 0) == y_first, y, z)
    return jnp.where(jnp.bitwise_and(place, bit) == 0, 1.0, -1.0).astype(F32)


def mix_kernel(step, value_ref, partner_ref, *outs):
    sign = my_sign(step)
    for i in range(value_ref.shape[1] // HB):
        part = pl.ds(i * HB, HB)
        total = value_ref[:, part].astype(F32) * sign + partner_ref[:, part].astype(F32)
        store_rows(total.astype(BF16), [out.at[:, part] for out in outs])


def mix(step, value, partner, rows):
    ff = value.shape[1]
    return call(
        functools.partial(mix_kernel, step),
        "mix",
        6,
        [VMEM] * 2,
        [VMEM] * len(rows),
        [pltpu.VMEM((count, ff), BF16) for count in rows],
    )(value, partner)


def rotate_kernel(step, table_ref, *refs):
    sign = my_sign(step)
    values, partners, rotated_ref = refs[: len(refs) // 2], refs[len(refs) // 2 : -1], refs[-1]
    for i in range(rotated_ref.shape[0] // HB):
        part = pl.ds(i * HB, HB)
        mixed = jnp.concatenate(
            [
                (value[:, part].astype(F32) * sign + partner[:, part].astype(F32)).astype(BF16)
                for value, partner in zip(values, partners)
            ]
        )
        turned = lax.dot_general(
            table_ref[...], mixed, (((1,), (1,)), ((), ())), preferred_element_type=F32
        )
        rotated_ref[part, :] = (turned * (1.0 / SCALE)).astype(BF16)


def rotate(table, step, values, partners):
    ff = values[0].shape[1]
    tokens = sum(value.shape[0] for value in values)
    return call(
        functools.partial(rotate_kernel, step),
        "rotate",
        8,
        [VMEM] * (1 + 2 * len(values)),
        VMEM,
        pltpu.VMEM((ff, tokens), BF16),
    )(table, *values, *partners)


def partial_sum(rotated, grads, part):
    left = jnp.concatenate([ref[part, :] for ref in rotated], axis=1)
    return jnp.dot(left, grads, preferred_element_type=F32)


def gather_rows(blocks, refs, all_grads):
    tokens = all_grads.shape[0] // len(blocks)
    for i, (which, row) in enumerate(blocks):
        all_grads[pl.ds(i * tokens, tokens), :] = refs[which][row * tokens : (row + 1) * tokens, :]


def early_kernel(blocks, *refs):
    count = len(blocks)
    rotated, grads, (out_ref, all_grads) = refs[:count], refs[count:-2], refs[-2:]
    gather_rows(blocks, grads, all_grads)
    for i in range(out_ref.shape[0] // HB):
        part = pl.ds(i * HB, HB)
        out_ref[part, :] = partial_sum(rotated, all_grads[...], part)


def early_product(rotated, blocks, grads):
    ff, tokens = rotated[0].shape
    cols = grads[0].shape[1]
    return call(
        functools.partial(early_kernel, blocks),
        "early_product",
        10,
        [VMEM] * (len(rotated) + len(grads)),
        VMEM,
        pltpu.VMEM((ff, cols), F32),
        [pltpu.VMEM((len(rotated) * tokens, cols), BF16)],
    )(*rotated, *grads)


def late_kernel(blocks, *refs):
    count = len(blocks)
    rotated, grads = refs[:count], refs[count:-6]
    keep_ref, early_ref, out_ref, all_grads, held, sems = refs[-6:]
    gather_rows(blocks, grads, all_grads)
    copies = []
    for i in range(early_ref.shape[0] // HB):
        part = pl.ds(i * HB, HB)
        total = early_ref[part, :] + partial_sum(rotated, all_grads[...], part)
        held[part, :] = jnp.where(keep_ref[part, :].astype(F32) > 0.0, total, 0.0).astype(BF16)
        copies.append(pltpu.make_async_copy(held.at[part, :], out_ref.at[part, :], sems.at[i]))
        copies[-1].start()
    for copy in copies:
        copy.wait()


def late_product(rotated, blocks, grads, keep, early):
    tokens = rotated[0].shape[1]
    return call(
        functools.partial(late_kernel, blocks),
        "late_product",
        14,
        [VMEM] * (len(rotated) + len(grads) + 2),
        ANY,
        jax.ShapeDtypeStruct(early.shape, BF16),
        [pltpu.VMEM((len(rotated) * tokens, early.shape[1]), BF16)] + streamed(*early.shape),
    )(*rotated, *grads, keep, early)


def place(stage):
    core, z, y = (lax.axis_index(axis) for axis in ("core", "z", "y"))
    return jnp.where((core == 0) == (stage == 0), y, z)


def quarter(index, rows):
    return pl.ds(pl.multiple_of(jnp.bitwise_and(index, 3) * rows, rows), rows)


def deal_kernel(stage, *refs):
    terms, outs = refs[:-4], refs[-4:]
    mine = place(stage)
    rows = outs[0].shape[0]
    for k, out in enumerate(outs):
        part_rows = quarter(mine + k, rows)
        for i in range(out.shape[1] // HB):
            part = pl.ds(i * HB, HB)
            out[:, part] = sum(ref[part_rows, part].astype(F32) for ref in terms).astype(BF16)


def deal(name, stage, *terms):
    tokens, ff = terms[0].shape
    return call(
        functools.partial(deal_kernel, stage),
        name,
        6,
        [VMEM] * len(terms),
        [VMEM] * 4,
        [pltpu.VMEM((tokens // 4, ff), BF16)] * 4,
    )(*terms)


def spread(pieces, stage):
    def route(distance):
        def to(x, c, z, y):
            if (c == 0) == (stage == 0):
                return (x, c, z, (y + distance) % 4)
            return (x, c, (z + distance) % 4, y)

        return to

    return [pieces[0]] + [move(pieces[k], route(k)) for k in BEHIND[1:]]


def mix_quarters_kernel(stage, *refs):
    values, outs = refs[:4], refs[4:]
    mine = place(stage)
    for k, out in enumerate(outs):
        signs = []
        for m in BEHIND:
            both = jnp.bitwise_and(jnp.bitwise_and(mine + k, mine - m), 3)
            odd = jnp.bitwise_and(both + (both >> 1), 1)
            signs.append((1 - 2 * odd).astype(F32))
        for i in range(out.shape[1] // HB):
            part = pl.ds(i * HB, HB)
            total = sum(ref[:, part].astype(F32) * sign for ref, sign in zip(values, signs))
            out[:, part] = total.astype(BF16)


def mix_quarters(stage, values):
    return call(
        functools.partial(mix_quarters_kernel, stage),
        "mix_quarters",
        6,
        [VMEM] * 4,
        [VMEM] * 4,
        [pltpu.VMEM(values[0].shape, BF16)] * 4,
    )(*values)


def collect_kernel(*refs):
    values, outs = refs[:4], refs[4:]
    rows = values[0].shape[0]
    if len(outs) == 1:
        for k, ref in zip(BEHIND, values):
            outs[0][quarter(place(1) - k, rows), :] = ref[...]
        return
    outs, held = outs[:4], outs[4]
    for k, ref in zip(BEHIND, values):
        held[quarter(place(0) - k, rows), :] = ref[...]
    for k, out in enumerate(outs):
        out[...] = held[quarter(place(1) + k, rows), :]


def collect(values, last):
    rows, ff = values[0].shape
    whole = (4 * rows, ff)
    return call(
        collect_kernel,
        "collect",
        6,
        [VMEM] * 4,
        VMEM if last else [VMEM] * 4,
        jax.ShapeDtypeStruct(whole, BF16) if last else [pltpu.VMEM((rows, ff), BF16)] * 4,
        [] if last else [pltpu.VMEM(whole, BF16)],
    )(*values)


def mix_axis(step):
    return 1 << (step // 2), step % 2 == 0


def partner(value, step):
    bit, y_first = mix_axis(step)

    def route(x, c, z, y):
        return (x, c, z, y ^ bit) if (c == 0) == y_first else (x, c, z ^ bit, y)

    return move(value, route)


def on_device(hidden, out_grad, weight, inv_scale):
    table = hadamard(HB)
    inv = inv_scale[None, :]
    tokens = hidden.shape[0]
    half = tokens // 2
    whole, halves = (tokens,), (half, half)

    kept, given = split(after(out_grad, table), weight.shape[1])
    got = partner(hidden, 0)
    to_opp, own, to_ahead = pair(kept, swap(given))
    opp, bwd = across(to_opp), forward(to_ahead)
    turned, keep = quantize(table, after(weight, own), inv)

    (hid,) = mix(0, after(hidden, turned), got, whole)
    got = partner(hid, 1)
    opp_mine, *opp_other = product([after(opp, hid)], (2 * tokens,), turned, whole + halves)
    opp_other = [swap(opp_other[j], 8 + j) for j in (0, 1)]
    (first_send,) = add("add_first", whole, opp_mine, opp_other)
    first = forward(first_send)
    own_mine, own_other = product([after(own, first_send)], (2 * tokens,), turned, whole * 2)
    own_other = swap(own_other, 1)
    (hid,) = mix(1, after(hid, own_mine), got, whole)
    got = partner(hid, 2)
    bwd = after(bwd, hid)
    fwd = [swap(bwd[(2 + j) * tokens : (3 + j) * tokens], 2 + j) for j in (0, 1)]
    *bwd_parts, fwd_other, fwd_mine, fwd_mine_rest = product(
        [bwd] + fwd, (2 * tokens, tokens, tokens), turned, halves * 2 + whole + halves
    )
    bwd_mine = [swap(bwd_parts[j], 4 + j) for j in (0, 1)]
    bwd_other = [swap(bwd_parts[2 + j], 6 + j) for j in (0, 1)]
    (own_sum,) = add("add_own", whole, after(own_mine, fwd_other), own_other)
    (third_send,) = add(
        "add_third",
        whole,
        after(first, own_sum),
        [fwd_mine, fwd_mine_rest],
        bwd_other,
        flops=THIRD_FLOPS,
    )
    third = forward(third_send)
    (second_send,) = add("add_second", whole, after(fwd_other, third_send), bwd_mine)
    second = forward_crossed(second_send)
    hid = list(mix(2, after(hid, second_send), got, halves))
    got = [partner(piece, 3) for piece in hid]
    rotated = rotate(table, 3, hid, got)
    pieces = deal("deal_grad", 0, own_sum, after(second, rotated), after(third, rotated))
    values = spread(pieces, 0)
    bwd_a, fwd_a = forward(rotated), backward(rotated)
    other = swap(rotated, 11)
    pieces = mix_quarters(0, [after(values[0], rotated)] + values[1:])
    values = spread(pieces, 0)
    pieces = collect([after(values[0], bwd_a, fwd_a)] + values[1:], False)
    opp_a = forward(bwd_a)
    fwd_b, bwd_b = swap(after(bwd_a, pieces[0]), 12), swap(after(fwd_a, pieces[0]), 13)
    values = spread(pieces, 1)
    early = early_product(
        [rotated, other, bwd_a, bwd_b, fwd_b, fwd_a],
        ((0, 0), (0, 1), (1, 0), (1, 1), (2, 0), (3, 0)),
        [own, bwd] + fwd,
    )
    pieces = mix_quarters(1, [after(values[0], early)] + values[1:])
    values = spread(pieces, 1)
    opp_a = after(opp_a, pieces[0])
    weight_grad = late_product(
        [opp_a, swap(opp_a, 14)], ((0, 0), (0, 1)), [opp], keep, early
    )
    hidden_grad = collect([after(values[0], weight_grad)] + values[1:], True)
    return hidden_grad, weight_grad


def solution(mesh):
    grid = jax.sharding.Mesh(mesh.devices.reshape(4, 2, 4, 4), AXES)
    dp, tensor = ("x", "core"), ("z", "y")
    in_specs = (P(dp, tensor), P(dp, None), P(tensor, dp), P(dp))
    out_specs = (P(dp, tensor), P(tensor, dp))
    return jax.shard_map(
        on_device, mesh=grid, in_specs=in_specs, out_specs=out_specs, check_vma=False
    )
```

```python
import functools

import jax
import jax.numpy as jnp
from jax import lax
from jax.experimental import pallas as pl
from jax.experimental.pallas import tpu as pltpu
from jax.sharding import PartitionSpec as P

HB = 256
SCALE = 64.0
THIRD_FLOPS = 2 * 10**9
BEHIND = (0, 2, 1, 3)
AXES = ("x", "core", "z", "y")
BF16 = jnp.bfloat16
F32 = jnp.float32
VMEM = pl.BlockSpec(memory_space=pltpu.VMEM)
ANY = pl.BlockSpec(memory_space=pl.ANY)


def move(value, route, turn=0):
    nx, nc, nz, ny = (lax.axis_size(axis) for axis in AXES)

    def flat(x, c, z, y):
        return ((x % nx * nc + c) * nz + z) * ny + y

    pairs = [
        (flat(x, c, z, y), flat(*route(x, c, z, y)))
        for x in range(nx)
        for c in range(nc)
        for z in range(nz)
        for y in range(ny)
    ]
    return lax.ppermute(value, AXES, pairs[turn:] + pairs[:turn])


def swap(value, turn=0):
    return move(value, lambda x, c, z, y: (x, 1 - c, z, y), turn)


def forward(value):
    return move(value, lambda x, c, z, y: (x + 1 - 2 * c, c, z, y))


def backward(value):
    return move(value, lambda x, c, z, y: (x - 1 + 2 * c, c, z, y))


def forward_crossed(value):
    return move(value, lambda x, c, z, y: (x + 1 - 2 * c, 1 - c, z, y))


def across(value):
    return move(value, lambda x, c, z, y: (x + 2, c, z, y))


def hadamard(order):
    i = jnp.arange(order, dtype=jnp.int32)
    both = jnp.bitwise_and(i[:, None], i[None, :])
    return (1 - 2 * (lax.population_count(both) % 2)).astype(BF16)


def after(value, *earlier):
    return lax.optimization_barrier((value,) + earlier)[0]


def in_hbm(value):
    return pltpu.with_memory_space_constraint(value, pltpu.HBM)


def call(kernel, name, mib, in_specs, out_specs, out_shape, scratch_shapes=(), grid=(), flops=1):
    return pl.pallas_call(
        kernel,
        grid=grid,
        in_specs=in_specs,
        out_specs=out_specs,
        out_shape=out_shape,
        scratch_shapes=scratch_shapes,
        compiler_params=pltpu.CompilerParams(vmem_limit_bytes=mib * 2**20),
        cost_estimate=pl.CostEstimate(flops=flops, bytes_accessed=1, transcendentals=0),
        name=name,
    )


def split_kernel(grad_ref, kept_ref, given_ref, sems):
    x, core = lax.axis_index("x"), lax.axis_index("core")
    cols = kept_ref.shape[-1]
    opposite, here = lax.rem(x + 2, 4), x
    ahead, back = lax.rem(x + 5 - 2 * core, 4), lax.rem(x + 3 + 2 * core, 4)
    kept = ((opposite, core), (here, core), (ahead, core), (ahead, 1 - core))
    given = ((opposite, 1 - core), (here, 1 - core), (back, 1 - core), (back, core))
    copies = []
    for out, blocks in ((kept_ref, kept), (given_ref, given)):
        for i, (chip, its_core) in enumerate(blocks):
            part = pl.ds(pl.multiple_of((chip * 2 + its_core) * cols, cols), cols)
            copies.append(
                pltpu.make_async_copy(grad_ref.at[:, part], out.at[i], sems.at[len(copies)])
            )
            copies[-1].start()
    for copy in copies:
        copy.wait()


def split(out_grad, cols):
    shape = pltpu.VMEM((4, out_grad.shape[0], cols), BF16)
    return call(
        split_kernel, "split", 4, [ANY], [ANY] * 2, [shape] * 2, [pltpu.SemaphoreType.DMA((8,))]
    )(in_hbm(out_grad))


def pair_kernel(kept_ref, got_ref, opp_ref, own_ref, ahead_ref):
    tokens = kept_ref.shape[1]
    for i, (ref, row) in enumerate(
        ((opp_ref, 0), (own_ref, 0), (ahead_ref, 0), (ahead_ref, 2 * tokens))
    ):
        ref[row : row + tokens, :] = kept_ref[i]
        ref[row + tokens : row + 2 * tokens, :] = got_ref[i]


def pair(kept, got):
    tokens, cols = kept.shape[1:]
    return call(
        pair_kernel,
        "pair",
        4,
        [VMEM, VMEM],
        [VMEM] * 3,
        [pltpu.VMEM((rows * tokens, cols), BF16) for rows in (2, 2, 4)],
    )(kept, got)


def store_rows(value, outs):
    row = 0
    for out in outs:
        out[...] = value[row : row + out.shape[0]]
        row += out.shape[0]


def stream(hbm_ref, held_ref, sems):
    copies = []
    for i in range(hbm_ref.shape[0] // HB):
        part = pl.ds(i * HB, HB)
        copies.append(pltpu.make_async_copy(hbm_ref.at[part, :], held_ref.at[part, :], sems.at[i]))
        copies[-1].start()
    return copies


def streamed(ff, cols):
    return [pltpu.VMEM((ff, cols), BF16), pltpu.SemaphoreType.DMA((ff // HB,))]


def quantize_kernel(table_ref, weight_ref, inv_ref, turned_ref, keep_ref, held, sems):
    copies = stream(weight_ref, held, sems)
    inv = inv_ref[...]
    step = (1.0 / SCALE) / inv
    for i, copy in enumerate(copies):
        part = pl.ds(i * HB, HB)
        copy.wait()
        raw_code = jnp.floor(held[part, :].astype(F32) * inv + 0.5)
        code = jnp.clip(raw_code, -8.0, 7.0)
        keep_ref[part, :] = jnp.where(raw_code == code, 1.0, 0.0).astype(BF16)
        turned = jnp.dot(table_ref[...], code.astype(BF16), preferred_element_type=F32)
        turned_ref[part, :] = (turned * step).astype(BF16)


def quantize(table, weight, inv):
    ff, cols = weight.shape
    return call(
        quantize_kernel,
        "quantize",
        14,
        [VMEM, ANY, VMEM],
        [VMEM] * 2,
        [pltpu.VMEM((ff, cols), BF16)] * 2,
        streamed(ff, cols),
    )(table, in_hbm(weight), inv)


def product_kernel(takes, *refs):
    grads, turned_ref, outs = refs[: len(takes)], refs[len(takes)], refs[len(takes) + 1 :]
    left = [ref[:rows, :] for ref, rows in zip(grads, takes)]
    left = left[0] if len(left) == 1 else jnp.concatenate(left)
    for i in range(turned_ref.shape[0] // HB):
        part = pl.ds(i * HB, HB)
        result = lax.dot_general(
            left, turned_ref[part, :], (((1,), (1,)), ((), ())), preferred_element_type=F32
        ).astype(BF16)
        store_rows(result, [out.at[:, part] for out in outs])


def product(grads, takes, turned, rows):
    ff = turned.shape[0]
    return call(
        functools.partial(product_kernel, takes),
        "product",
        10,
        [VMEM] * (len(grads) + 1),
        [VMEM] * len(rows),
        [pltpu.VMEM((size, ff), BF16) for size in rows],
    )(*grads, turned)


def add_kernel(first_rows, pieces, *refs):
    outs = refs[sum(pieces) :]
    terms, start = [], 0
    for count in pieces:
        terms.append(refs[start : start + count])
        start += count
    height = sum(out.shape[0] for out in outs)
    for i in range(outs[0].shape[1] // HB):
        part = pl.ds(i * HB, HB)
        total = None
        for row, term in zip(first_rows, terms):
            value = [ref[:, part] if len(term) > 1 else ref[row : row + height, part] for ref in term]
            value = value[0] if len(value) == 1 else jnp.concatenate(value)
            value = value.astype(F32)
            total = value if total is None else total + value
        store_rows(total.astype(BF16), [out.at[:, part] for out in outs])


def add(name, rows, *terms, flops=1):
    first_rows = [term[1] if isinstance(term, tuple) else 0 for term in terms]
    terms = [
        term if isinstance(term, list) else [term[0] if isinstance(term, tuple) else term]
        for term in terms
    ]
    ff = terms[0][0].shape[1]
    flat = [piece for term in terms for piece in term]
    return call(
        functools.partial(add_kernel, tuple(first_rows), tuple(len(term) for term in terms)),
        name,
        6,
        [VMEM] * len(flat),
        [VMEM] * len(rows),
        [pltpu.VMEM((count, ff), BF16) for count in rows],
        flops=flops,
    )(*flat)


def my_sign(step):
    core, z, y = (lax.axis_index(axis) for axis in ("core", "z", "y"))
    bit, y_first = mix_axis(step)
    place = jnp.where((core == 0) == y_first, y, z)
    return jnp.where(jnp.bitwise_and(place, bit) == 0, 1.0, -1.0).astype(F32)


def mix_kernel(step, value_ref, partner_ref, *outs):
    sign = my_sign(step)
    for i in range(value_ref.shape[1] // HB):
        part = pl.ds(i * HB, HB)
        total = value_ref[:, part].astype(F32) * sign + partner_ref[:, part].astype(F32)
        store_rows(total.astype(BF16), [out.at[:, part] for out in outs])


def mix(step, value, partner, rows):
    ff = value.shape[1]
    return call(
        functools.partial(mix_kernel, step),
        "mix",
        6,
        [VMEM] * 2,
        [VMEM] * len(rows),
        [pltpu.VMEM((count, ff), BF16) for count in rows],
    )(value, partner)


def rotate_kernel(step, table_ref, *refs):
    sign = my_sign(step)
    values, partners, rotated_ref = refs[: len(refs) // 2], refs[len(refs) // 2 : -1], refs[-1]
    for i in range(rotated_ref.shape[0] // HB):
        part = pl.ds(i * HB, HB)
        mixed = jnp.concatenate(
            [
                (value[:, part].astype(F32) * sign + partner[:, part].astype(F32)).astype(BF16)
                for value, partner in zip(values, partners)
            ]
        )
        turned = lax.dot_general(
            table_ref[...], mixed, (((1,), (1,)), ((), ())), preferred_element_type=F32
        )
        rotated_ref[part, :] = (turned * (1.0 / SCALE)).astype(BF16)


def rotate(table, step, values, partners):
    ff = values[0].shape[1]
    tokens = sum(value.shape[0] for value in values)
    return call(
        functools.partial(rotate_kernel, step),
        "rotate",
        8,
        [VMEM] * (1 + 2 * len(values)),
        VMEM,
        pltpu.VMEM((ff, tokens), BF16),
    )(table, *values, *partners)


def partial_sum(rotated, grads, part):
    left = jnp.concatenate([ref[part, :] for ref in rotated], axis=1)
    return jnp.dot(left, grads, preferred_element_type=F32)


def gather_rows(blocks, refs, all_grads):
    tokens = all_grads.shape[0] // len(blocks)
    for i, (which, row) in enumerate(blocks):
        all_grads[pl.ds(i * tokens, tokens), :] = refs[which][row * tokens : (row + 1) * tokens, :]


def early_kernel(blocks, *refs):
    count = len(blocks)
    rotated, grads, (out_ref, all_grads) = refs[:count], refs[count:-2], refs[-2:]
    gather_rows(blocks, grads, all_grads)
    for i in range(out_ref.shape[0] // HB):
        part = pl.ds(i * HB, HB)
        out_ref[part, :] = partial_sum(rotated, all_grads[...], part)


def early_product(rotated, blocks, grads):
    ff, tokens = rotated[0].shape
    cols = grads[0].shape[1]
    return call(
        functools.partial(early_kernel, blocks),
        "early_product",
        10,
        [VMEM] * (len(rotated) + len(grads)),
        VMEM,
        pltpu.VMEM((ff, cols), F32),
        [pltpu.VMEM((len(rotated) * tokens, cols), BF16)],
    )(*rotated, *grads)


def late_kernel(blocks, *refs):
    count = len(blocks)
    rotated, grads = refs[:count], refs[count:-6]
    keep_ref, early_ref, out_ref, all_grads, held, sems = refs[-6:]
    gather_rows(blocks, grads, all_grads)
    copies = []
    for i in range(early_ref.shape[0] // HB):
        part = pl.ds(i * HB, HB)
        total = early_ref[part, :] + partial_sum(rotated, all_grads[...], part)
        held[part, :] = jnp.where(keep_ref[part, :].astype(F32) > 0.0, total, 0.0).astype(BF16)
        copies.append(pltpu.make_async_copy(held.at[part, :], out_ref.at[part, :], sems.at[i]))
        copies[-1].start()
    for copy in copies:
        copy.wait()


def late_product(rotated, blocks, grads, keep, early):
    tokens = rotated[0].shape[1]
    return call(
        functools.partial(late_kernel, blocks),
        "late_product",
        14,
        [VMEM] * (len(rotated) + len(grads) + 2),
        ANY,
        jax.ShapeDtypeStruct(early.shape, BF16),
        [pltpu.VMEM((len(rotated) * tokens, early.shape[1]), BF16)] + streamed(*early.shape),
    )(*rotated, *grads, keep, early)


def place(stage):
    core, z, y = (lax.axis_index(axis) for axis in ("core", "z", "y"))
    return jnp.where((core == 0) == (stage == 0), y, z)


def quarter(index, rows):
    return pl.ds(pl.multiple_of(jnp.bitwise_and(index, 3) * rows, rows), rows)


def deal_kernel(stage, *refs):
    terms, outs = refs[:-4], refs[-4:]
    mine = place(stage)
    rows = outs[0].shape[0]
    for k, out in enumerate(outs):
        part_rows = quarter(mine + k, rows)
        for i in range(out.shape[1] // HB):
            part = pl.ds(i * HB, HB)
            out[:, part] = sum(ref[part_rows, part].astype(F32) for ref in terms).astype(BF16)


def deal(name, stage, *terms):
    tokens, ff = terms[0].shape
    return call(
        functools.partial(deal_kernel, stage),
        name,
        6,
        [VMEM] * len(terms),
        [VMEM] * 4,
        [pltpu.VMEM((tokens // 4, ff), BF16)] * 4,
    )(*terms)


def spread(pieces, stage):
    def route(distance):
        def to(x, c, z, y):
            if (c == 0) == (stage == 0):
                return (x, c, z, (y + distance) % 4)
            return (x, c, (z + distance) % 4, y)

        return to

    return [pieces[0]] + [move(pieces[k], route(k)) for k in BEHIND[1:]]


def mix_quarters_kernel(stage, *refs):
    values, outs = refs[:4], refs[4:]
    mine = place(stage)
    signs = []
    for k in range(4):
        row = []
        for m in BEHIND:
            both = jnp.bitwise_and(jnp.bitwise_and(mine + k, mine - m), 3)
            odd = jnp.bitwise_and(both + (both >> 1), 1)
            row.append((1 - 2 * odd).astype(F32))
        signs.append(row)
    for i in range(outs[0].shape[1] // HB):
        part = pl.ds(i * HB, HB)
        blocks = [ref[:, part].astype(F32) for ref in values]
        for out, row in zip(outs, signs):
            out[:, part] = sum(block * sign for block, sign in zip(blocks, row)).astype(BF16)


def mix_quarters(stage, values):
    return call(
        functools.partial(mix_quarters_kernel, stage),
        "mix_quarters",
        6,
        [VMEM] * 4,
        [VMEM] * 4,
        [pltpu.VMEM(values[0].shape, BF16)] * 4,
    )(*values)


def collect_kernel(*refs):
    values, outs = refs[:4], refs[4:]
    rows = values[0].shape[0]
    if len(outs) == 1:
        for k, ref in zip(BEHIND, values):
            outs[0][quarter(place(1) - k, rows), :] = ref[...]
        return
    outs, held = outs[:4], outs[4]
    for k, ref in zip(BEHIND, values):
        held[quarter(place(0) - k, rows), :] = ref[...]
    for k, out in enumerate(outs):
        out[...] = held[quarter(place(1) + k, rows), :]


def collect(values, last):
    rows, ff = values[0].shape
    whole = (4 * rows, ff)
    return call(
        collect_kernel,
        "collect",
        6,
        [VMEM] * 4,
        VMEM if last else [VMEM] * 4,
        jax.ShapeDtypeStruct(whole, BF16) if last else [pltpu.VMEM((rows, ff), BF16)] * 4,
        [] if last else [pltpu.VMEM(whole, BF16)],
    )(*values)


def mix_axis(step):
    return 1 << (step // 2), step % 2 == 0


def partner(value, step):
    bit, y_first = mix_axis(step)

    def route(x, c, z, y):
        return (x, c, z, y ^ bit) if (c == 0) == y_first else (x, c, z ^ bit, y)

    return move(value, route)


def on_device(hidden, out_grad, weight, inv_scale):
    table = hadamard(HB)
    inv = inv_scale[None, :]
    tokens = hidden.shape[0]
    half = tokens // 2
    whole, halves = (tokens,), (half, half)

    kept, given = split(after(out_grad, table), weight.shape[1])
    got = partner(hidden, 0)
    to_opp, own, to_ahead = pair(kept, swap(given))
    opp, bwd = across(to_opp), forward(to_ahead)
    turned, keep = quantize(table, after(weight, own), inv)

    (hid,) = mix(0, after(hidden, turned), got, whole)
    got = partner(hid, 1)
    opp_mine, *opp_other = product([after(opp, hid)], (2 * tokens,), turned, whole + halves)
    opp_other = [swap(opp_other[j], 8 + j) for j in (0, 1)]
    (first_send,) = add("add_first", whole, opp_mine, opp_other)
    first = forward(first_send)
    own_mine, own_other = product([after(own, first_send)], (2 * tokens,), turned, whole * 2)
    own_other = swap(own_other, 1)
    (hid,) = mix(1, after(hid, own_mine), got, whole)
    got = partner(hid, 2)
    bwd = after(bwd, hid)
    fwd = [swap(bwd[(2 + j) * tokens : (3 + j) * tokens], 2 + j) for j in (0, 1)]
    *bwd_parts, fwd_other, fwd_mine, fwd_mine_rest = product(
        [bwd] + fwd, (2 * tokens, tokens, tokens), turned, halves * 2 + whole + halves
    )
    bwd_mine = [swap(bwd_parts[j], 4 + j) for j in (0, 1)]
    bwd_other = [swap(bwd_parts[2 + j], 6 + j) for j in (0, 1)]
    (own_sum,) = add("add_own", whole, after(own_mine, fwd_other), own_other)
    (third_send,) = add(
        "add_third",
        whole,
        after(first, own_sum),
        [fwd_mine, fwd_mine_rest],
        bwd_other,
        flops=THIRD_FLOPS,
    )
    third = forward(third_send)
    (second_send,) = add("add_second", whole, after(fwd_other, third_send), bwd_mine)
    second = forward_crossed(second_send)
    hid = list(mix(2, after(hid, second_send), got, halves))
    got = [partner(piece, 3) for piece in hid]
    rotated = rotate(table, 3, hid, got)
    pieces = deal("deal_grad", 0, own_sum, after(second, rotated), after(third, rotated))
    values = spread(pieces, 0)
    bwd_a, fwd_a = forward(rotated), backward(rotated)
    other = swap(rotated, 11)
    pieces = mix_quarters(0, [after(values[0], rotated)] + values[1:])
    values = spread(pieces, 0)
    pieces = collect([after(values[0], bwd_a, fwd_a)] + values[1:], False)
    opp_a = forward(bwd_a)
    fwd_b, bwd_b = swap(after(bwd_a, pieces[0]), 12), swap(after(fwd_a, pieces[0]), 13)
    values = spread(pieces, 1)
    early = early_product(
        [rotated, other, bwd_a, bwd_b, fwd_b, fwd_a],
        ((0, 0), (0, 1), (1, 0), (1, 1), (2, 0), (3, 0)),
        [own, bwd] + fwd,
    )
    pieces = mix_quarters(1, [after(values[0], early)] + values[1:])
    values = spread(pieces, 1)
    opp_a = after(opp_a, pieces[0])
    weight_grad = late_product(
        [opp_a, swap(opp_a, 14)], ((0, 0), (0, 1)), [opp], keep, early
    )
    hidden_grad = collect([after(values[0], weight_grad)] + values[1:], True)
    return hidden_grad, weight_grad


def solution(mesh):
    grid = jax.sharding.Mesh(mesh.devices.reshape(4, 2, 4, 4), AXES)
    dp, tensor = ("x", "core"), ("z", "y")
    in_specs = (P(dp, tensor), P(dp, None), P(tensor, dp), P(dp))
    out_specs = (P(dp, tensor), P(tensor, dp))
    return jax.shard_map(
        on_device, mesh=grid, in_specs=in_specs, out_specs=out_specs, check_vma=False
    )
```
